32 devices in a mesh: row: 4 (over z), col: 8 (over y, x, core).
Axes of the slice: x: 2, y: 2, z: 4, core: 2. Of those that a mesh axis runs over, the one named last changes fastest.
Arguments:
- patches: bfloat16 [8, 16, 32, 768], P('col', 'row'), may hold values from -6 to 6
- pixel_grads: bfloat16 [8, 16, 32, 768], P('col', 'row'), may hold values from -6 to 6
- widths: int32 [8], P('col'), may hold values from 8 to 32, as said below
- patch_mask: int32 [8, 16, 32], P('col'), may hold values from 0 to 1, as said below
- heads_weight: float32 [768, 2304], P('col'), may hold values from -0.21875 to 0.21875
- heads_first: float32 [768, 2304], P('col'), may hold values from -192 to 192
- heads_second: float32 [768, 2304], P('col'), may hold values from 1024 to 4096
- merge_weight: float32 [768, 768], P('col'), may hold values from -1.75 to 1.75
- merge_first: float32 [768, 768], P('col'), may hold values from -96 to 96
- merge_second: float32 [768, 768], P('col'), may hold values from 256 to 1024
- expand_weight: float32 [768, 3072], P('col'), may hold values from -0.21875 to 0.21875
- expand_first: float32 [768, 3072], P('col'), may hold values from -96 to 96
- expand_second: float32 [768, 3072], P('col'), may hold values from 256 to 1024
- shrink_weight: float32 [3072, 768], P('col'), may hold values from -0.109375 to 0.109375
- shrink_first: float32 [3072, 768], P('col'), may hold values from -192 to 192
- shrink_second: float32 [3072, 768], P('col'), may hold values from 1024 to 4096
- kernel_weight: float32 [9, 768, 768], P(None, 'col'), may hold values from -0.078125 to 0.078125
- kernel_first: float32 [9, 768, 768], P(None, 'col'), may hold values from -256 to 256
- kernel_second: float32 [9, 768, 768], P(None, 'col'), may hold values from 2048 to 8192
- norm_table: float32 [4, 768], P(None, 'col'), may hold values from -1 to 2, as said below
- norm_first: float32 [4, 768], P(None, 'col'), may hold values from -384 to 384
- norm_second: float32 [4, 768], P(None, 'col'), may hold values from 4096 to 16384
Outputs:
- pixels: bfloat16 [8, 16, 32, 768], P('col', 'row')
- patch_gradient: float32 [8, 16, 32, 768], P('col', 'row')
- heads_gradient: float32 [768, 2304], P('col')
- heads_mean: float32 [768, 2304], P('col')
- heads_square: float32 [768, 2304], P('col')
- heads_master: float32 [768, 2304], P('col')
- heads_copy: bfloat16 [768, 2304], P('col')
- merge_gradient: float32 [768, 768], P('col')
- merge_mean: float32 [768, 768], P('col')
- merge_square: float32 [768, 768], P('col')
- merge_master: float32 [768, 768], P('col')
- merge_copy: bfloat16 [768, 768], P('col')
- expand_gradient: float32 [768, 3072], P('col')
- expand_mean: float32 [768, 3072], P('col')
- expand_square: float32 [768, 3072], P('col')
- expand_master: float32 [768, 3072], P('col')
- expand_copy: bfloat16 [768, 3072], P('col')
- shrink_gradient: float32 [3072, 768], P('col')
- shrink_mean: float32 [3072, 768], P('col')
- shrink_square: float32 [3072, 768], P('col')
- shrink_master: float32 [3072, 768], P('col')
- shrink_copy: bfloat16 [3072, 768], P('col')
- kernel_gradient: float32 [9, 768, 768], P(None, 'col')
- kernel_mean: float32 [9, 768, 768], P(None, 'col')
- kernel_square: float32 [9, 768, 768], P(None, 'col')
- kernel_master: float32 [9, 768, 768], P(None, 'col')
- kernel_copy: bfloat16 [9, 768, 768], P(None, 'col')
- norm_gradient: float32 [4, 768], P(None, 'col')
- norm_mean: float32 [4, 768], P(None, 'col')
- norm_square: float32 [4, 768], P(None, 'col')
- norm_master: float32 [4, 768], P(None, 'col')
- norm_copy: bfloat16 [4, 768], P(None, 'col')
The draws below stay inside these ranges and needn't reach their ends.
Inputs may be any that keep to these rules, and one draw needn't show every extreme that they name: Grid widths lie from 8 to 32; in every draw some image has 32 columns and another 32 // 4. `patch_mask`: the first slot (row 0, column 0) of every image is 1. `norm_table`: rows 0 and 2 are gains within 0.7 to 1.3, rows 1 and 3 shifts within -0.9 to 0.9.
All inputs are finite; a program needn't handle non-finite values.
Results may differ from the reference program's by a relative error of at most 0.012.
The reference program's roundings to bfloat16 on the way count: a program that leaves them out, or rounds other values in their place, can miss the bound.
Values may be sent and summed in bfloat16 or wider, within the bound.
A program may use at most 256 MiB of HBM per device.

```python
import math
import jax
import jax.numpy as jnp
from jax import lax

D = 768
HEADS = 12
HEAD_DIM = 64
FF = 3072
GRID_W = 32
STEP = 5
GRID_H = 16
IMAGES = 8
TOKENS = 4096


def draw_widths(key, part):
    key = jax.random.fold_in(key, 11)
    first_key, second_key = jax.random.split(key)
    grid_spans = jax.random.randint(first_key, (IMAGES,), GRID_W // 4, GRID_W + 1)
    shuffled = jax.random.permutation(second_key, IMAGES)
    grid_spans = grid_spans.at[shuffled[0]].set(GRID_W)
    grid_spans = grid_spans.at[shuffled[1]].set(GRID_W // 4)
    return grid_spans.astype(jnp.int32)


def draw_patch_mask(key, part):
    key = jax.random.fold_in(key, 12)
    levels = jax.random.randint(key, (IMAGES, GRID_H, GRID_W), 0, 8)
    marked = jnp.where(levels > 0, 1, 0).astype(jnp.int32)
    return marked.at[:, 0, 0].set(1)


def draw_norm_table(key, part):
    key = jax.random.fold_in(key, 13)
    first_key, second_key = jax.random.split(key)
    gain_spread = jax.random.uniform(first_key, (2, D), jnp.float32, -1.0, 1.0)
    shifts = 0.3 * jnp.clip(jax.random.normal(second_key, (2, D), jnp.float32), -3.0, 3.0)
    table = jnp.stack([1.0 + 0.3 * gain_spread[0], shifts[0], 1.0 + 0.3 * gain_spread[1], shifts[1]])
    return table.astype(jnp.float32)


def block_levels(stream_key, dims, pieces, least, high):
    gain = 1.0
    for axis_at, shards_of in pieces:
        steps = jax.random.uniform(jax.random.fold_in(jax.random.fold_in(stream_key, 6), axis_at), (shards_of,), jnp.float32, least / len(pieces), high / len(pieces))
        gain = gain * jnp.repeat(jnp.exp(steps), dims[axis_at] // shards_of).reshape((-1,) + (1,) * (len(dims) - 1 - axis_at))
    return gain


def gaussian(stream_key, dims, width, most, shards=(), kind=jnp.bfloat16):
    result = width * jax.random.normal(stream_key, dims, jnp.float32)
    if shards:
        result = result * block_levels(stream_key, dims, shards, -0.22, 0.18)
    return jnp.clip(result, -most, most).astype(kind)


def setup_inputs(seed: int = 0) -> dict:
    streams_of = jax.random.split(jax.random.key(seed), 23)
    patches = gaussian(streams_of[0], (IMAGES, GRID_H, GRID_W, D), 1.0, 6.0, ((0, 8), (1, 4)))
    pixel_grads = gaussian(streams_of[1], (IMAGES, GRID_H, GRID_W, D), 1.0, 6.0, ((0, 8), (1, 4)))
    widths = draw_widths(jax.random.fold_in(streams_of[22], 71), 0)
    patch_mask = draw_patch_mask(jax.random.fold_in(streams_of[22], 71), 0)
    heads_weight = gaussian(streams_of[4], (D, 3 * D), D ** -0.5, 0.21875, ((0, 8),), jnp.float32)
    heads_first = gaussian(streams_of[5], (D, 3 * D), ((TOKENS // 4) ** 0.5), 192.0, ((0, 8),), jnp.float32)
    heads_second = jnp.clip(jnp.exp(math.log(4096.0) - 1.3862944 * jax.random.uniform(streams_of[6], (D, 3 * D), jnp.float32) ** block_levels(streams_of[6], (D, 3 * D), ((0, 8),), -0.2, 0.2)), 1024.0, 4096.0)
    merge_weight = gaussian(streams_of[7], (D, D), (D // 64) ** -0.5, 1.75, ((0, 8),), jnp.float32)
    merge_first = gaussian(streams_of[8], (D, D), ((TOKENS // 16) ** 0.5), 96.0, ((0, 8),), jnp.float32)
    merge_second = jnp.clip(jnp.exp(math.log(1024.0) - 1.3862944 * jax.random.uniform(streams_of[9], (D, D), jnp.float32) ** block_levels(streams_of[9], (D, D), ((0, 8),), -0.2, 0.2)), 256.0, 1024.0)
    expand_weight = gaussian(streams_of[10], (D, FF), D ** -0.5, 0.21875, ((0, 8),), jnp.float32)
    expand_first = gaussian(streams_of[11], (D, FF), ((TOKENS // 16) ** 0.5), 96.0, ((0, 8),), jnp.float32)
    expand_second = jnp.clip(jnp.exp(math.log(1024.0) - 1.3862944 * jax.random.uniform(streams_of[12], (D, FF), jnp.float32) ** block_levels(streams_of[12], (D, FF), ((0, 8),), -0.2, 0.2)), 256.0, 1024.0)
    shrink_weight = gaussian(streams_of[13], (FF, D), FF ** -0.5, 0.109375, ((0, 8),), jnp.float32)
    shrink_first = gaussian(streams_of[14], (FF, D), ((TOKENS // 4) ** 0.5), 192.0, ((0, 8),), jnp.float32)
    shrink_second = jnp.clip(jnp.exp(math.log(4096.0) - 1.3862944 * jax.random.uniform(streams_of[15], (FF, D), jnp.float32) ** block_levels(streams_of[15], (FF, D), ((0, 8),), -0.2, 0.2)), 1024.0, 4096.0)
    kernel_weight = gaussian(streams_of[16], (9, D, D), (9 * D) ** -0.5, 0.078125, ((1, 8),), jnp.float32)
    kernel_first = gaussian(streams_of[17], (9, D, D), ((TOKENS // 2) ** 0.5), 256.0, ((1, 8),), jnp.float32)
    kernel_second = jnp.clip(jnp.exp(math.log(8192.0) - 1.3862944 * jax.random.uniform(streams_of[18], (9, D, D), jnp.float32) ** block_levels(streams_of[18], (9, D, D), ((1, 8),), -0.2, 0.2)), 2048.0, 8192.0)
    norm_table = draw_norm_table(jax.random.fold_in(streams_of[22], 71), 0)
    norm_first = gaussian(streams_of[20], (4, D), (TOKENS ** 0.5), 384.0, ((1, 8),), jnp.float32)
    norm_second = jnp.clip(jnp.exp(math.log(16384.0) - 1.3862944 * jax.random.uniform(streams_of[21], (4, D), jnp.float32) ** block_levels(streams_of[21], (4, D), ((1, 8),), -0.2, 0.2)), 4096.0, 16384.0)
    return {"patches": patches, "pixel_grads": pixel_grads, "widths": widths, "patch_mask": patch_mask, "heads_weight": heads_weight, "heads_first": heads_first, "heads_second": heads_second, "merge_weight": merge_weight, "merge_first": merge_first, "merge_second": merge_second, "expand_weight": expand_weight, "expand_first": expand_first, "expand_second": expand_second, "shrink_weight": shrink_weight, "shrink_first": shrink_first, "shrink_second": shrink_second, "kernel_weight": kernel_weight, "kernel_first": kernel_first, "kernel_second": kernel_second, "norm_table": norm_table, "norm_first": norm_first, "norm_second": norm_second}


@jax.custom_vjp
def low(v):
    return lax.optimization_barrier(v.astype(jnp.bfloat16)).astype(jnp.float32)

@jax.custom_vjp
def low_back(v):
    return v

def low_keep(v):
    return (low(v), None)

def low_pass(kept, grad):
    return (grad,)

def back_keep(v):
    return (v, None)

def back_low(kept, grad):
    return (low(grad),)
low.defvjp(low_keep, low_pass)
low_back.defvjp(back_keep, back_low)
highest = lax.Precision.HIGHEST
beta_first = 0.5
beta_second = 0.5

def layer_norm(values, norm_gain, norm_shift):
    center = values - lax.optimization_barrier(jnp.mean(values, axis=-1, keepdims=True))
    spread = lax.optimization_barrier(jnp.mean(center * center, axis=-1, keepdims=True))
    return center * lax.rsqrt(spread + 1e-05) * norm_gain + norm_shift

def valid_cells(widths, patch_mask):
    column = jnp.arange(patch_mask.shape[-1], dtype=jnp.int32)
    inside = column[None, None, :] < widths[:, None, None]
    return jnp.logical_and(inside, patch_mask == 1)

def step_rates():
    return (D ** (-0.5), 8.0 * D ** (-0.5), D ** (-0.5), FF ** (-0.5), (9 * D) ** (-0.5), 0.3)

def adam_update(master, moment_one, moment_two, gradient, step_rate):
    new_mean = beta_first * moment_one + (1.0 - beta_first) * gradient
    new_square = beta_second * moment_two + (1.0 - beta_second) * gradient * gradient
    mean_hat = new_mean / (1.0 - beta_first ** STEP)
    square_hat = new_square / (1.0 - beta_second ** STEP)
    new_master = master - step_rate * (mean_hat / (jnp.sqrt(square_hat) + 1e-08) + 0.01 * master)
    return (gradient, new_mean, new_square, new_master, new_master.astype(jnp.bfloat16))

def decoder_group(patch_block, usable, heads_full, merge_full, expand_full, shrink_full, kernel_full, norm_full):
    images, grid_rows, grid_cols, model_width = patch_block.shape
    length = grid_rows * grid_cols
    tokens = patch_block.reshape(images, length, model_width)
    key_valid = usable.reshape(images, length)
    normed = low(layer_norm(tokens, norm_full[0], norm_full[1]))
    projected = low(low_back(jnp.einsum('ntc,cj->ntj', normed, heads_full, precision=highest)))
    query_heads = projected[:, :, :model_width].reshape(images, length, HEADS, HEAD_DIM)
    key_heads = projected[:, :, model_width:2 * model_width].reshape(images, length, HEADS, HEAD_DIM)
    value_heads = projected[:, :, 2 * model_width:].reshape(images, length, HEADS, HEAD_DIM)
    scores = low_back(0.125 * jnp.einsum('nqhd,nkhd->nhqk', query_heads, key_heads, precision=highest))
    scores = jnp.where(key_valid[:, None, None, :], scores, -1e+30)
    weights = jax.nn.softmax(scores, axis=-1)
    attended = jnp.einsum('nhqk,nkhd->nqhd', low(weights), value_heads, precision=highest)
    attended = low_back(low(attended)).reshape(images, length, model_width)
    after_attend = tokens + low_back(jnp.einsum('ntc,cd->ntd', attended, merge_full, precision=highest))
    normed_two = low(layer_norm(after_attend, norm_full[2], norm_full[3]))
    hidden = low_back(jnp.einsum('ntc,cf->ntf', normed_two, expand_full, precision=highest))
    active = low(jax.nn.gelu(hidden, approximate=False))
    after_feed = after_attend + low_back(jnp.einsum('ntf,fd->ntd', active, shrink_full, precision=highest))
    cell_values = low(after_feed).reshape(images, grid_rows, grid_cols, model_width)
    cell_values = cell_values * usable[..., None].astype(jnp.float32)
    padded = jnp.pad(cell_values, ((0, 0), (1, 1), (1, 1), (0, 0)))
    pixels = jnp.zeros(cell_values.shape, jnp.float32)
    for kernel_tap in range(9):
        row_step = kernel_tap // 3
        col_step = kernel_tap % 3
        window = padded[:, row_step:row_step + grid_rows, col_step:col_step + grid_cols]
        pixels = pixels + jnp.einsum('nyxc,cd->nyxd', window, kernel_full[kernel_tap], precision=highest)
    return pixels

def reference(patches, pixel_grads, widths, patch_mask, heads_weight, heads_first, heads_second, merge_weight, merge_first, merge_second, expand_weight, expand_first, expand_second, shrink_weight, shrink_first, shrink_second, kernel_weight, kernel_first, kernel_second, norm_table, norm_first, norm_second):
    usable = valid_cells(widths, patch_mask)
    cells_each = GRID_H * GRID_W
    group_size = math.gcd(IMAGES, max(1, 4096 // cells_each))
    usable_stack = usable.reshape(IMAGES // group_size, group_size, GRID_H, GRID_W)
    checked = jax.checkpoint(decoder_group)

    def forward(patch_values, heads_full, merge_full, expand_full, shrink_full, kernel_full, norm_full):
        stacked = patch_values.reshape(IMAGES // group_size, group_size, GRID_H, GRID_W, D)

        def advance(state_carry, scan_item):
            return (state_carry, checked(scan_item[0], scan_item[1], heads_full, merge_full, expand_full, shrink_full, kernel_full, norm_full))
        _, pixel_stack = lax.scan(advance, jnp.zeros((), jnp.float32), (stacked, usable_stack))
        return pixel_stack.reshape(IMAGES, GRID_H, GRID_W, D)
    masters = (heads_weight, merge_weight, expand_weight, shrink_weight, kernel_weight, norm_table)
    lowered = [master.astype(jnp.bfloat16).astype(jnp.float32) for master in masters]
    pixels, pull_back = jax.vjp(forward, patches.astype(jnp.float32), *lowered)
    gradients = pull_back(pixel_grads.astype(jnp.float32))
    rates = step_rates()
    heads_out = adam_update(heads_weight, heads_first, heads_second, gradients[1], rates[0])
    merge_out = adam_update(merge_weight, merge_first, merge_second, gradients[2], rates[1])
    expand_out = adam_update(expand_weight, expand_first, expand_second, gradients[3], rates[2])
    shrink_out = adam_update(shrink_weight, shrink_first, shrink_second, gradients[4], rates[3])
    kernel_out = adam_update(kernel_weight, kernel_first, kernel_second, gradients[5], rates[4])
    norm_out = adam_update(norm_table, norm_first, norm_second, gradients[6], rates[5])
    return (pixels.astype(jnp.bfloat16), gradients[0], heads_out[0], heads_out[1], heads_out[2], heads_out[3], heads_out[4], merge_out[0], merge_out[1], merge_out[2], merge_out[3], merge_out[4], expand_out[0], expand_out[1], expand_out[2], expand_out[3], expand_out[4], shrink_out[0], shrink_out[1], shrink_out[2], shrink_out[3], shrink_out[4], kernel_out[0], kernel_out[1], kernel_out[2], kernel_out[3], kernel_out[4], norm_out[0], norm_out[1], norm_out[2], norm_out[3], norm_out[4])
```

```python
import functools
import types

import jax
import jax.numpy as jnp
from jax import lax
from jax.experimental import pallas as pl
from jax.experimental.pallas import tpu as pltpu
from jax.sharding import PartitionSpec as P

D = 768
HEADS = 12
HEAD_DIM = 64
FF = 3072
STEP = 5
TEAM = 8

beta_first = 0.5
beta_second = 0.5

MESH = pl.DeviceIdType.MESH
F32 = jnp.float32
BF16 = jnp.bfloat16


def layer_norm(values, norm_gain, norm_shift):
    center = values - jnp.mean(values, axis=-1, keepdims=True)
    spread = jnp.mean(center * center, axis=-1, keepdims=True)
    return center * lax.rsqrt(spread + 1e-05) * norm_gain + norm_shift


def exact_gelu(values):
    return jax.nn.gelu(values, approximate=False)


def step_rates():
    return (D ** (-0.5), 8.0 * D ** (-0.5), D ** (-0.5), FF ** (-0.5), (9 * D) ** (-0.5), 0.3)


def adam_body(plan, counts, *refs):
    params, passed = counts
    taken = 4 * params + 4 + passed
    given, results = refs[:taken], refs[taken : taken + 5 * params + 5 + passed]
    scratch = refs[taken + len(results) :]
    in_sem, out_sem = scratch[-2:]
    norm_in, norm_out = given[4 * params : 4 * params + 4], results[5 * params : 5 * params + 5]
    through = [
        pltpu.make_async_copy(src, dst, out_sem.at[len(plan), at])
        for at, (src, dst) in enumerate(zip(given[4 * params + 4 :], results[5 * params + 5 :]))
    ]

    def cut(ref, taps):
        return ref if taps is None else ref.at[pl.ds(*taps)]

    loads = []
    for at, (param, taps) in enumerate(plan):
        grads, values, _ = scratch[3 * at : 3 * at + 3]
        into = [grads] + [values.at[index] for index in range(3)]
        made = [
            pltpu.make_async_copy(cut(ref, taps), dst, in_sem.at[at, index])
            for index, (ref, dst) in enumerate(zip(given[4 * param : 4 * param + 4], into))
        ]
        for each in made:
            each.start()
        loads.append(made)
    for each in through:
        each.start()
    rates = step_rates()
    gradient = norm_in[0][pl.ds(0, 4), pl.ds(0, norm_in[1].shape[1])]
    updated = adam_update(norm_in[1][...], norm_in[2][...], norm_in[3][...], gradient, rates[5])
    for ref, value in zip(norm_out, updated):
        ref[...] = value
    stores = []
    for at, (param, taps) in enumerate(plan):
        grads, values, copies = scratch[3 * at : 3 * at + 3]
        for each in loads[at]:
            each.wait()
        rows, columns = grads.shape[-2:]
        deep = 16 if rows % 16 == 0 else rows
        wide = D if columns % D == 0 else columns
        leads = range(grads.shape[0]) if grads.ndim == 3 else (None,)

        def update(step, carry):
            inside = pl.ds(pl.multiple_of(step * deep, deep), deep) if deep < rows else slice(None)
            for lead in leads:
                for begin in range(0, columns, wide):
                    spot = (inside, pl.ds(begin, wide))
                    spot = spot if lead is None else (lead,) + spot
                    updated = adam_update(
                        *(values[(index,) + spot] for index in range(3)),
                        grads[spot].astype(F32),
                        rates[param],
                    )
                    for index, value in zip((3, 1, 2, 0), updated):
                        values[(index,) + spot] = value
                    copies[spot] = updated[4]
            return carry

        if deep < rows:
            lax.fori_loop(0, rows // deep, update, 0)
        else:
            update(0, 0)
        sources = [values.at[index] for index in (3, 1, 2, 0)] + [copies]
        for index, src in enumerate(sources):
            dst = cut(results[5 * param + index], taps)
            made = pltpu.make_async_copy(src, dst, out_sem.at[at, index])
            made.start()
            stores.append(made)
    for each in stores + through:
        each.wait()


def adam_all(params, norm, passed):
    plan = []
    for at, (_, master, _, _) in enumerate(params):
        if master.ndim == 3:
            plan += [(at, (tap, 3)) for tap in range(0, master.shape[0], 3)]
        else:
            plan.append((at, None))
    plan.sort(key=lambda block: -params[block[0]][1].size)
    any_at, vmem = pl.BlockSpec(memory_space=pl.ANY), pl.BlockSpec(memory_space=pltpu.VMEM)
    results = [
        jax.ShapeDtypeStruct(group[1].shape, dtype)
        for group in [*params, norm]
        for dtype in (F32, F32, F32, F32, BF16)
    ] + [jax.ShapeDtypeStruct(array.shape, array.dtype) for array in passed]
    scratch = []
    for at, taps in plan:
        grads, master = params[at][:2]
        shape = master.shape if taps is None else (taps[1],) + master.shape[1:]
        scratch += [
            pltpu.VMEM(shape, grads.dtype),
            pltpu.VMEM((4,) + shape, F32),
            pltpu.VMEM(shape, BF16),
        ]
    flat = [array for group in params for array in group]
    return pl.pallas_call(
        functools.partial(adam_body, plan, (len(params), len(passed))),
        out_shape=results,
        in_specs=[any_at] * len(flat) + [vmem] * 4 + [any_at] * len(passed),
        out_specs=[any_at] * (5 * len(params)) + [vmem] * 5 + [any_at] * len(passed),
        scratch_shapes=scratch
        + [
            pltpu.SemaphoreType.DMA((len(plan), 4)),
            pltpu.SemaphoreType.DMA((len(plan) + 1, 5)),
        ],
        compiler_params=pltpu.CompilerParams(vmem_limit_bytes=60 << 20),
        cost_estimate=pl.CostEstimate(
            flops=20 * sum(group[1].size for group in params),
            bytes_accessed=30 * sum(group[1].size for group in params),
            transcendentals=0,
        ),
        name="adam",
    )(*flat, *norm, *passed)


def adam_update(master, moment_one, moment_two, gradient, step_rate):
    new_mean = beta_first * (moment_one + gradient)
    new_square = beta_second * (moment_two + gradient * gradient)
    square_hat = new_square * (1.0 / (1.0 - beta_second**STEP))
    root = square_hat * lax.rsqrt(square_hat) + 1e-08
    inverse = pl.reciprocal(root, approx=True)
    inverse = inverse * (2.0 - root * inverse)
    toward = new_mean * inverse
    new_master = master * (1.0 - 0.01 * step_rate) - toward * (
        step_rate / (1.0 - beta_first**STEP)
    )
    return (gradient, new_mean, new_square, new_master, new_master.astype(jnp.bfloat16))


def dot(a, b, dims):
    return lax.dot_general(a, b, (dims, ((), ())), preferred_element_type=F32)


def place():
    teams = lax.axis_size("col") // TEAM
    row, col = lax.axis_index("row"), lax.axis_index("col")
    at, team = col // teams, col % teams

    def device(row_at, chip_at, core_at):
        return (row_at, (chip_at * 2 + core_at) * teams + team)

    return row, at // 2, at % 2, device


def dot_in(a, b):
    return dot(a, b, ((1,), (0,)))


def dot_right(a, b):
    return dot(a, b, ((1,), (1,)))


def dot_left(a, b):
    return dot(a, b, ((0,), (0,)))


def greet(devices):
    barrier = pltpu.get_barrier_semaphore()
    for device in devices:
        pl.semaphore_signal(barrier, inc=1, device_id=device, device_id_type=MESH)
    return lambda: pl.semaphore_wait(barrier, len(devices))


KINDS = (
    "patches",
    "heads",
    "norm",
    "grads",
    "usable",
    "merge",
    "expand",
    "attended",
    "rim_up",
    "rim_down",
    "normed_two",
    "down",
    "feed",
    "normed_two_grad",
    "expand_back",
    "cells",
    "above",
    "below",
    "attended_grad",
    "merge_back",
    "normed_in",
    "normed_over",
    "normed_out",
    "pixels",
    "heads_back",
    "heads_rows",
    "norm_back",
    "norm_rows",
)
PAIRS = (
    "grads",
    "cells",
    "heads",
    "merge",
    "expand",
    "kernel",
    "shrink",
    "shrink_back",
    "expand_back",
    "merge_back",
    "heads_back",
)


def layer_body(sizes, names, *refs):
    rows, half, share, grid_cols, heads_here = sizes
    v = types.SimpleNamespace(**dict(zip(names, refs)))
    row, quad, core, device_at = place()
    sibling = device_at(row, quad, 1 - core)
    team = 2 * half
    at = quad * 2 + core
    local, width = v.patches.shape
    length = rows * local
    block = width // half
    head_part = width // rows
    own_rows = half * share
    is_end = jnp.logical_or(row == 0, row == rows - 1)
    is_middle = jnp.logical_not(is_end)
    toward = jnp.where(row < rows // 2, 1, -1)
    inner = device_at(lax.rem(row + toward + rows, rows), quad, core)
    outer = device_at(lax.rem(row - toward + rows, rows), quad, core)

    def turn(base, step, count):
        return lax.rem(base + count + step, count)

    def across(step):
        return (quad, quad + 1 - 2 * (quad % 2), quad + 2 - 4 * (quad // 2), 3 - quad)[step]

    def on_chip(step, shift=0):
        return device_at(turn(row, shift, rows), across(step), core)

    def on_row(step):
        return device_at(turn(row, step, rows), quad, core)

    def on_team(step):
        there = turn(at, step, team)
        return device_at(row, there // 2, lax.rem(there, 2))

    all_here = greet(
        [on_team(step) for step in range(1, team)]
        + [on_row(step) for step in range(1, rows)]
        + [on_chip(step, shift) for shift in (-1, 1) for step in range(half)]
    )

    started = []

    def link(kind, index, src, dst, device):
        return pltpu.make_async_remote_copy(
            src_ref=src,
            dst_ref=dst,
            send_sem=v.send_sem.at[KINDS.index(kind), index],
            recv_sem=v.recv_sem.at[KINDS.index(kind), index],
            device_id=device,
            device_id_type=MESH,
        )

    def pair(kind, index, src, dst):
        return pltpu.make_async_remote_copy(
            src_ref=src,
            dst_ref=dst,
            send_sem=v.pair_send.at[PAIRS.index(kind), index],
            recv_sem=v.pair_recv.at[PAIRS.index(kind), index],
            device_id=sibling,
            device_id_type=MESH,
        )

    def start(made):
        made.start()
        started.append(made)
        return made

    def arrived(made):
        for each in made:
            each.wait_recv()

    def gone(made):
        for each in made:
            each.wait_send()
            started[:] = [other for other in started if other is not each]

    def to_chips(kind, src, dst):
        return [
            start(link(kind, step, src(across(step)), dst(step), on_chip(step)))
            for step in range(1, half)
        ]

    def to_rows(kind, src, dst):
        return [
            start(link(kind, step, src(turn(row, step, rows)), dst, on_row(step)))
            for step in range(1, rows)
        ]

    def share_of(ref, chip, core_at):
        return ref.at[pl.ds(pl.multiple_of((chip * 2 + core_at) * share, share), share)]

    def line(kind, j, src, dst, device):
        return pltpu.make_async_remote_copy(
            src_ref=src,
            dst_ref=dst,
            send_sem=v.line_send.at[kind, j],
            recv_sem=v.line_recv.at[kind, j],
            device_id=device,
            device_id_type=MESH,
        )

    chunks = v.line_got.shape[0]

    def line_inward(j):
        return line(0, j, v.line_got.at[j], v.line_got.at[j], inner)

    def line_over(j):
        return line(1, j, v.line_got.at[j], line_result(j), inner)

    def line_result(j):
        if j < half:
            return v.shrink_here.at[pl.ds(j * share, share)]
        if j < 2 * half:
            return v.expand_sum.at[j - half]
        if j < chunks - 1:
            return v.kernel_here.at[j - 2 * half]
        return v.merge_here

    def line_outward(j):
        return line(2, j, line_result(j), line_result(j), outer)

    ready, done_in, done_over = [], [0], [0]

    def line_ready(j, value):
        @pl.when(is_end)
        def _():
            v.line_got[j] = value().astype(BF16)
            line_inward(j).start()

        ready.append((j, value))

    def line_step(count=1):
        for _ in range(count):
            if done_in[0] < len(ready):
                j, value = ready[done_in[0]]
                done_in[0] += 1

                @pl.when(is_middle)
                def _():
                    line_inward(j).wait_recv()
                    v.line_got[j] = (value() + v.line_got[j].astype(F32)).astype(BF16)
                    line_over(j).start()

            behind = 2 if done_in[0] < chunks else 0
            if done_over[0] + behind <= done_in[0] and done_over[0] < done_in[0]:
                k = ready[done_over[0]][0]
                done_over[0] += 1

                @pl.when(is_middle)
                def _():
                    line_over(k).wait_recv()
                    total = v.line_got[k].astype(F32) + line_result(k)[...].astype(F32)
                    line_result(k)[...] = total.astype(BF16)
                    line_outward(k).start()

    def fetch(index, src, dst):
        made = pltpu.make_async_copy(src, dst, v.own_sem.at[index])
        made.start()
        return made

    heads_in = [
        fetch(
            3 + half + part,
            v.heads.at[:, pl.ds(part * width, width)],
            v.slope.at[part, pl.ds(0, share)],
        )
        for part in range(3)
    ]
    kernel_in = fetch(0, v.kernel, v.kernel_kept)
    merge_in = fetch(1, v.merge, v.slope.at[half - 1, pl.ds(0, share)])
    expand_in = [
        fetch(2 + chip, v.expand.at[:, pl.ds(chip * width, width)], v.expand_kept.at[chip])
        for chip in range(half)
    ]
    shrink_in = fetch(2 + half, v.shrink, v.grad.at[pl.ds(0, own_rows)])
    v.patches_all[row] = v.patches[...]
    v.grads_all[0] = v.grads[...]
    extent = v.widths[0]
    column = lax.broadcasted_iota(jnp.int32, (1, grid_cols), 1)
    corner = lax.broadcasted_iota(jnp.int32, (grid_cols, grid_cols), 0)
    corner = corner == lax.broadcasted_iota(jnp.int32, (grid_cols, grid_cols), 1)

    def usable_row(y):
        held = jnp.logical_and(v.patch_mask[pl.ds(y, 1), :] == 1, column < extent)
        return jnp.where(held, 1.0, 0.0)

    grid_rows = local // grid_cols
    for y in range(rows * grid_rows):
        v.key_valid[:, pl.ds(y * grid_cols, grid_cols)] = usable_row(y)
    for y in range(grid_rows):
        turned = jnp.where(corner, usable_row(row * grid_rows + y), 0.0)
        turned = jnp.sum(turned, axis=1, keepdims=True)
        v.usable[pl.ds(y * grid_cols, grid_cols), :] = jnp.broadcast_to(
            turned, (grid_cols, 128)
        ).astype(BF16)
    v.usable_all[0] = v.usable[...]
    v.norm_low[...] = jnp.zeros_like(v.norm_low)
    v.norm_low[pl.ds(0, 4), pl.ds(0, share)] = v.norm_table[...].astype(BF16).astype(F32)
    v.norm_got[at] = v.norm_low[...]
    for each in heads_in:
        each.wait()
    for there in range(rows):

        @pl.when(row == there)
        def _():
            for part in range(3):
                taken = v.slope[part, pl.ds(0, share), pl.ds(there * head_part, head_part)]
                v.heads_low[:, pl.ds(part * head_part, head_part)] = taken.astype(BF16)

    taps = 9 * share
    wide_taps = v.kernel_all.shape[1]
    kernel_in.wait()
    for tap in range(9):
        v.kernel_all[core, pl.ds(tap * share, share), :] = v.kernel_kept[tap].astype(BF16)
    padding = jnp.zeros((wide_taps - taps, width), BF16)
    for side in range(2):
        v.kernel_all[side, pl.ds(taps, wide_taps - taps), :] = padding

    all_here()
    patches_sent = to_rows("patches", lambda there: v.patches, v.patches_all.at[row])
    mine = v.kernel_all.at[core, pl.ds(0, taps)]
    kernel_sent = start(pair("kernel", 0, mine, mine))
    grads_sent = to_chips("grads", lambda there: v.grads, v.grads_all.at.__getitem__)

    def spread(kind, src, ref):
        mine = share_of(ref, quad, core)
        sent = to_chips(kind, src, lambda step: mine)
        mine[...] = src(quad)[...]
        forward = [start(pair(kind, 0, mine, mine))]
        return sent, forward

    def forwarded(kind, ref, spreading):
        sent, forward = spreading
        for step in range(1, half):
            sent[step - 1].wait_recv()
            there = share_of(ref, across(step), core)
            forward.append(start(pair(kind, step, there, there)))
        return forward

    heads_sent = spread("heads", lambda there: v.heads_low, v.heads_all)
    norm_sent = [
        start(link("norm", step, v.norm_low, v.norm_got.at[at], on_team(step)))
        for step in range(1, team)
    ]
    usable_sent = to_chips("usable", lambda there: v.usable, v.usable_all.at.__getitem__)
    merge_in.wait()
    v.merge_low[...] = v.slope[half - 1, pl.ds(0, share)].astype(BF16)
    merge_sent = spread("merge", lambda there: v.merge_low, v.merge_all)
    for chip in range(half):
        expand_in[chip].wait()
        v.expand_send[chip] = v.expand_kept[chip].astype(BF16)
    expand_sent = spread("expand", lambda there: v.expand_send.at[there], v.expand_all)
    shrink_mine = pl.ds(pl.multiple_of(core * own_rows, own_rows), own_rows)
    shrink_in.wait()
    v.shrink_all[shrink_mine, :] = v.grad[pl.ds(0, own_rows), :].astype(BF16)
    mine = v.shrink_all.at[shrink_mine]
    shrink_sent = start(pair("shrink", 0, mine, mine))

    tall = local + 2 * grid_cols
    spot = lax.rem(lax.broadcasted_iota(jnp.int32, (tall, block), 0), grid_cols)
    not_first, not_last = spot != 0, spot != grid_cols - 1

    def rim(b, slot, begin, size, lane=0, lanes=block):
        rows_at, lanes_at = slot // 2 * tall + begin, slot % 2 * (length // 2) + lane
        return b, pl.ds(rows_at, size), pl.ds(lanes_at, lanes)

    def pixels_back(first, last):
        count = last - first
        here = v.grads_all[pl.ds(first, count)].reshape(count * local, width)
        empty = jnp.zeros((2 * grid_cols, block), F32)
        for slot in range(count):
            for b in range(3):
                v.probs[rim(b, slot, local, 2 * grid_cols)] = empty
        for side in range(2):
            every = dot_right(here, v.kernel_all[side])
            for tap in range(9):
                a, b = tap // 3, tap % 3
                term = every[:, tap * share : (tap + 1) * share].reshape(count, local, share)
                for slot in range(count):
                    into = rim(b, slot, a * grid_cols, local, side * share, share)
                    if a == 0:
                        v.probs[into] = term[slot]
                    else:
                        v.probs[into] += term[slot]
        for slot in range(first, last):
            ahead, center, back = (v.probs[rim(b, slot - first, 0, tall)] for b in range(3))
            ahead = jnp.where(not_first, ahead, 0.0)
            back = jnp.where(not_last, back, 0.0)
            whole = (
                center
                + jnp.concatenate([ahead[1:], ahead[:1]], axis=0)
                + jnp.concatenate([back[tall - 1 :], back[: tall - 1]], axis=0)
            )
            v.rim_up_send[slot] = whole[:grid_cols].astype(BF16)
            v.rim_down_send[slot] = whole[tall - grid_cols :].astype(BF16)
            v.feed_part[slot] = whole[grid_cols : tall - grid_cols]

    kernel_sent.wait_recv()
    pixels_back(0, 1)
    arrived(grads_sent)
    grads_pair = start(pair("grads", 0, v.grads_all, v.grads_other))
    pixels_back(1, half)
    rims = [
        start(link("rim_up", 0, v.rim_up_send, v.rim_below, on_row(-1))),
        start(link("rim_down", 0, v.rim_down_send, v.rim_above, on_row(1))),
    ]

    heads_done = forwarded("heads", v.heads_all, heads_sent)
    arrived(norm_sent)
    for there in range(team):
        v.gains[:, pl.ds(there * share, share)] = v.norm_got[there, :, pl.ds(0, share)]

    def normal(values):
        center = values - jnp.mean(values, axis=-1, keepdims=True)
        spread_here = jnp.mean(center * center, axis=-1, keepdims=True)
        scale = lax.rsqrt(spread_here + 1e-05)
        return center * scale, scale

    arrived(patches_sent)
    for there in range(rows):
        hat, _ = normal(v.patches_all[there].astype(F32))
        normed = (hat * v.gains[0:1] + v.gains[1:2]).astype(BF16)
        v.normed[pl.ds(there * local, local), :] = normed
    arrived(heads_done)
    v.projected[...] = dot_in(v.normed[...], v.heads_all[...]).astype(BF16)

    def part_of(ref, part, head):
        return ref[:, pl.ds(part * head_part + head * HEAD_DIM, HEAD_DIM)]

    def attend(there):
        inside = pl.ds(pl.multiple_of(there * local, local), local)
        for head in range(heads_here):
            queries = v.projected[inside, pl.ds(head * HEAD_DIM, HEAD_DIM)]
            queries = queries * jnp.asarray(0.125, BF16)
            scores = dot_right(queries, part_of(v.projected, 1, head))
            scores = jnp.where(v.key_valid[...] > 0.0, scores, -1e30)
            risen = jnp.exp(scores - jnp.max(scores, axis=-1, keepdims=True))
            probs = risen * (1.0 / jnp.sum(risen, axis=-1, keepdims=True))
            v.probs[head, inside, :] = probs
            taken = dot_in(probs.astype(BF16), part_of(v.projected, 2, head))
            v.attended_send[there, :, pl.ds(head * HEAD_DIM, HEAD_DIM)] = taken.astype(BF16)

    attended_sent = []
    for step in range(1, rows):
        there = turn(row, step, rows)
        attend(there)
        src, dst = v.attended_send.at[there], v.attended_got.at[row]
        attended_sent.append(start(link("attended", step, src, dst, on_row(step))))
        if step == 2:
            arrived(usable_sent)
            arrived(rims)
            for slot in range(half):
                first, last = pl.ds(0, grid_cols), pl.ds(local - grid_cols, grid_cols)
                above = jnp.where(row > 0, v.rim_above[slot].astype(F32), 0.0)
                below = jnp.where(row < rows - 1, v.rim_below[slot].astype(F32), 0.0)
                v.feed_part[slot, first, :] += above
                v.feed_part[slot, last, :] += below
                kept = v.usable_all[slot, :, pl.ds(0, 1)].astype(F32) > 0.0
                v.down_got[quad, slot] = jnp.where(kept, v.feed_part[slot], 0.0).astype(BF16)
            down_sent = to_chips(
                "down", lambda there: v.down_got.at[quad], lambda step: v.down_got.at[quad]
            )
    attend(row)
    v.attended_got[row] = v.attended_send[row]
    merge_done = forwarded("merge", v.merge_all, merge_sent)
    expand_done = forwarded("expand", v.expand_all, expand_sent)

    v.normed_turned[...] = v.normed[...].T
    arrived(attended_sent)
    for there in range(rows):
        v.attended[:, pl.ds(there * head_part, head_part)] = v.attended_got[there]
    arrived(merge_done)
    after_attend = v.patches[...].astype(F32) + dot_in(v.attended[...], v.merge_all[...])
    v.after_attend[...] = after_attend
    hat, _ = normal(after_attend)
    v.normed_two[0] = (hat * v.gains[2:3] + v.gains[3:4]).astype(BF16)
    normed_two_sent = to_chips(
        "normed_two", lambda there: v.normed_two.at[0], v.normed_two.at.__getitem__
    )

    arrived(expand_done)
    shrink_sent.wait_recv()

    def stack(ref, first, last):
        return ref[pl.ds(first, last - first)].reshape((last - first) * local, ref.shape[-1])

    def place_in(ref, first, last, value):
        ref[pl.ds(first, last - first)] = value.reshape(last - first, local, ref.shape[-1])

    def forward(first, last):
        hidden = dot_in(stack(v.normed_two, first, last), v.expand_all[...])
        below = 0.5 * (1.0 + lax.erf(hidden * (0.5**0.5)))
        density = jnp.exp(-0.5 * hidden * hidden) * ((2.0 * 3.141592653589793) ** -0.5)
        place_in(v.slope, first, last, below + hidden * density)
        place_in(v.active, first, last, (hidden * below).astype(BF16))
        whole = dot_in(stack(v.active, first, last), v.shrink_all[...])
        place_in(v.feed_send, first, last, whole.astype(BF16))

    def backward(first, last):
        grad_here = dot_right(stack(v.down_in, first, last), v.shrink_all[...])
        grad_here = (grad_here * stack(v.slope, first, last)).astype(BF16)
        place_in(v.hidden_grad, first, last, grad_here)
        whole = dot_right(stack(v.hidden_grad, first, last), v.expand_all[...])
        place_in(v.normed_two_send, first, last, whole.astype(BF16))

    def send_back(kind, send, got, steps=(1, 2, 3)):
        if 1 in steps:
            got[0] = send[0]
        return [
            start(link(kind, step, send.at[step], got.at[step], on_chip(step)))
            for step in steps
        ]

    def flat(ref):
        return stack(ref, 0, half)

    v.attended_turned[...] = v.attended[...].T
    forward(0, 1)
    arrived(down_sent)
    for slot in range(half):
        for chip in range(half):
            v.down_in[slot, :, pl.ds(chip * block, block)] = v.down_got[chip, across(chip ^ slot)]
    backward(0, 1)
    arrived(normed_two_sent[:2])
    forward(1, half - 1)
    feed_sent = send_back("feed", v.feed_send, v.feed_got, (1, 2))
    arrived(normed_two_sent[2:])
    forward(half - 1, half)
    feed_sent += send_back("feed", v.feed_send, v.feed_got, (3,))
    v.grad[...] = dot_left(flat(v.active), flat(v.down_in))
    at_other = pl.multiple_of((1 - core) * own_rows, own_rows)
    v.shrink_send[...] = v.grad[pl.ds(at_other, own_rows), :].astype(BF16)
    shrink_back = start(pair("shrink_back", 0, v.shrink_send, v.shrink_got))
    backward(1, half)
    shrink_back.wait_recv()
    for j in range(half):

        def shrink_chunk(j=j):
            begin = pl.multiple_of(core * own_rows + j * share, share)
            inside = pl.ds(j * share, share)
            return v.grad[pl.ds(begin, share), :] + v.shrink_got[inside, :].astype(F32)

        line_ready(j, shrink_chunk)

    def split(value, kept, sent, lanes=slice(None)):
        for chip in range(half):
            begin = 2 * chip * share
            first, second = value[begin : begin + share], value[begin + share : begin + 2 * share]
            kept[chip, :, lanes] = jnp.where(core == 0, first, second)
            sent[chip] = jnp.where(core == 0, second, first).astype(BF16)

    arrived(feed_sent)
    after_feed = v.after_attend[...] + jnp.sum(v.feed_got[...].astype(F32), axis=0)
    kept = v.usable[:, pl.ds(0, 1)].astype(F32) > 0.0
    cells_here = jnp.where(kept, after_feed, 0.0).astype(BF16)
    for chip in range(half):
        v.cells_send[chip] = cells_here[:, chip * block : (chip + 1) * block]
    v.cells_got[0] = v.cells_send[quad]
    cells_sent = to_chips(
        "cells", lambda there: v.cells_send.at[there], v.cells_got.at.__getitem__
    )
    for step in range(half):
        there = across(step)
        head = v.cells_send.at[there, pl.ds(0, grid_cols)]
        foot = v.cells_send.at[there, pl.ds(local - grid_cols, grid_cols)]
        dst = v.below_got.at[step]
        cells_sent.append(start(link("below", step, head, dst, on_chip(step, -1))))
        dst = v.above_got.at[step]
        cells_sent.append(start(link("above", step, foot, dst, on_chip(step, 1))))
    normed_two_back = send_back("normed_two_grad", v.normed_two_send, v.normed_two_got)
    gone(expand_sent[0])
    split(dot_left(flat(v.normed_two), flat(v.hidden_grad)), v.expand_kept, v.expand_send)
    expand_pair = start(pair("expand_back", 0, v.expand_send, v.expand_got))

    line_step()

    expand_pair.wait_recv()
    for j in range(half):
        line_ready(half + j, lambda j=j: v.expand_kept[j] + v.expand_got[j].astype(F32))
    line_step()

    def lay_out(center, store):
        ahead = jnp.concatenate([center[tall - 1 :], center[: tall - 1]], axis=0)
        back = jnp.concatenate([center[1:], center[:1]], axis=0)
        shifts = (
            jnp.where(not_first[:, :share], ahead, 0.0).astype(BF16),
            center.astype(BF16),
            jnp.where(not_last[:, :share], back, 0.0).astype(BF16),
        )
        for tap in range(9):
            begin = tap // 3 * grid_cols
            store(pl.ds(tap * share, share), shifts[tap % 3][begin : begin + local])
        store(pl.ds(taps, wide_taps - taps), jnp.zeros((local, wide_taps - taps), BF16))

    arrived(cells_sent)
    for slot in range(half):
        over = jnp.where(row > 0, v.above_got[slot].astype(F32), 0.0)
        under = jnp.where(row < rows - 1, v.below_got[slot].astype(F32), 0.0)
        center = jnp.concatenate([over, v.cells_got[slot].astype(F32), under], axis=0)
        sides = (center[:, :share], center[:, share:])
        v.cells_pair[slot] = jnp.where(core == 0, sides[1], sides[0]).astype(BF16)
        for side in range(2):

            def store(lanes, value):
                v.window[side, slot, :, lanes] = value

            lay_out(sides[side], store)
        if slot % 2:
            line_step()
    cells_pair = start(pair("cells", 0, v.cells_pair, v.cells_other))

    def norm_back(hat, scale, gain, grad):
        inside = grad * gain
        mean = jnp.mean(inside, axis=-1, keepdims=True)
        along = jnp.mean(inside * hat, axis=-1, keepdims=True)
        return scale * (inside - mean - hat * along)

    arrived(normed_two_back)
    normed_two_grad = jnp.sum(v.normed_two_got[...].astype(F32), axis=0)
    hat, scale = normal(v.after_attend[...])
    v.norm_here[pl.ds(2, 1), :] = jnp.sum(normed_two_grad * hat, axis=0, keepdims=True)
    v.norm_here[pl.ds(3, 1), :] = jnp.sum(normed_two_grad, axis=0, keepdims=True)
    attend_part = norm_back(hat, scale, v.gains[2:3], normed_two_grad)
    attend_grad = v.down_in[0].astype(F32) + attend_part
    v.attend_grad[...] = attend_grad
    branch_in = attend_grad.astype(BF16)
    attended_grad = dot_right(branch_in, v.merge_all[...]).astype(BF16)
    for there in range(rows):
        begin = there * head_part
        v.attended_grad_send[there] = attended_grad[:, begin : begin + head_part]
    v.attended_grad_got[row] = v.attended_grad_send[row]
    attended_back = to_rows(
        "attended_grad",
        lambda there: v.attended_grad_send.at[there],
        v.attended_grad_got.at[row],
    )
    grads_pair.wait_recv()
    cells_pair.wait_recv()
    for slot in range(half):

        def store(lanes, value):
            v.window_other[slot, :, lanes] = value

        lay_out(v.cells_other[slot].astype(F32), store)
    line_step()

    for group in range(0, 9, 4):
        begin, end = group * share, min((group + 4) * share, wide_taps)
        lanes = pl.ds(begin, end - begin)
        mine = v.window[core, :, :, lanes].reshape(half * local, end - begin)
        other = v.window_other[:, :, lanes].reshape(half * local, end - begin)
        whole = dot_left(mine, flat(v.grads_all)) + dot_left(other, flat(v.grads_other))
        for tap in range(group, min(group + 4, 9)):
            at_tap = (tap - group) * share
            v.kernel_kept[tap] = whole[at_tap : at_tap + share]
            line_ready(2 * half + tap, lambda tap=tap: v.kernel_kept[tap])
        line_step()
    merge_kept, merge_send, merge_got = (
        ref.at[:, pl.ds(0, share)] for ref in (v.slope, v.hidden_grad, v.active)
    )
    heads_kept = (slice(None), slice(None), pl.ds(0, 3 * head_part))
    split(dot_in(v.attended_turned[...], branch_in), merge_kept, merge_send)
    merge_pair = start(pair("merge_back", 0, merge_send, merge_got))
    line_step()
    merge_pair.wait_recv()
    gone([merge_pair])
    merge_send[...] = (merge_kept[...] + merge_got[...].astype(F32)).astype(BF16)
    v.merge_pieces[quad] = merge_send[quad]
    merge_back = to_chips(
        "merge_back",
        lambda there: merge_send.at[there],
        lambda step: v.merge_pieces.at[quad],
    )
    arrived(attended_back)
    for head in range(heads_here):
        lanes = pl.ds(head * HEAD_DIM, HEAD_DIM)
        queries, keys, values = (part_of(v.projected, part, head) for part in range(3))
        branch = v.attended_grad_got[:, :, lanes].reshape(length, HEAD_DIM)
        query_grads = []
        for piece in range(rows):
            inside = pl.ds(piece * local, local)
            probs = v.probs[head, inside, :]
            prob_grad = dot_right(branch[piece * local : (piece + 1) * local], values)
            inner_sum = jnp.sum(probs * prob_grad, axis=-1, keepdims=True)
            scored = (probs * (prob_grad - inner_sum)).astype(BF16)
            v.score_grad[inside, :] = scored
            query_grads.append(0.125 * dot_in(scored, keys))
        query_grad = jnp.concatenate(query_grads, axis=0)
        key_grad = 0.125 * dot_left(queries, v.score_grad[...]).T
        value_grad = dot_left(branch, v.probs[head].astype(BF16)).T
        for part, value in enumerate((query_grad, key_grad, value_grad)):
            into = pl.ds(part * head_part + head * HEAD_DIM, HEAD_DIM)
            v.projected_grad[:, into] = value.astype(BF16)
        line_step(2)

    gone(normed_two_back)

    def along(for_end, for_middle):
        return turn(row, toward * jnp.where(is_end, for_end, for_middle), 2 * rows) % rows

    far, over, near = along(3, 2), along(2, 1), along(1, -1)

    def normed_piece(there):
        inside = pl.ds(pl.multiple_of(there * local, local), local)
        v.normed_two_send[there] = dot_right(v.projected_grad[inside, :], v.heads_all[...]).astype(
            BF16
        )

    def normed_in(index, there):
        src, dst = v.normed_two_send.at[there], v.patches_all.at[index]
        return link("normed_in", index, src, dst, inner)

    def normed_over(index, there):
        src, dst = v.normed_two_send.at[there], v.normed_two_got.at[index]
        return link("normed_over", index, src, dst, inner)

    def normed_out():
        src, dst = v.normed_two_send.at[near], v.patches_all.at[rows - 1]
        return link("normed_out", 0, src, dst, outer)

    for index, there in enumerate((far, over, near)):
        normed_piece(there)

        @pl.when(is_end)
        def _():
            normed_in(index, there).start()

    normed_piece(row)

    def normed_across():
        @pl.when(is_middle)
        def _():
            for index, there in enumerate((far, over)):
                normed_in(index, there).wait_recv()
                total = v.normed_two_send[there].astype(F32) + v.patches_all[index].astype(F32)
                v.normed_two_send[there] = total.astype(BF16)
                normed_over(index, there).start()

    def normed_outward():
        @pl.when(is_middle)
        def _():
            normed_over(0, far).wait_recv()
            total = v.normed_two_send[near].astype(F32) + v.normed_two_got[0].astype(F32)
            v.normed_two_send[near] = total.astype(BF16)
            normed_out().start()

    assert done_in[0] >= 2 * half
    split(dot_in(v.normed_turned[...], v.projected_grad[...]), v.expand_kept, v.heads_send, heads_kept[2])
    heads_pair = start(pair("heads_back", 0, v.heads_send, v.heads_got))
    normed_across()
    line_step()
    heads_pair.wait_recv()
    gone([heads_pair])
    v.heads_send[...] = (v.expand_kept[heads_kept] + v.heads_got[...].astype(F32)).astype(BF16)
    v.heads_pieces[quad] = v.heads_send[quad]
    heads_back = to_chips(
        "heads_back",
        lambda there: v.heads_send.at[there],
        lambda step: v.heads_pieces.at[quad],
    )
    line_step()
    normed_outward()

    assert done_over[0] >= 2 * half

    @pl.when(is_end)
    def _():
        for j in range(half, 2 * half):
            line_outward(j).wait_recv()

    v.expand_pieces[quad] = v.expand_sum[quad]
    expand_back = to_chips(
        "expand_back",
        lambda there: v.expand_sum.at[there],
        lambda step: v.expand_pieces.at[quad],
    )

    gone(feed_sent)
    for first in range(0, half, 2):
        cells = v.window[:, pl.ds(first, 2)].reshape(2, 2 * local, wide_taps)
        whole = dot_in(cells[0], v.kernel_all[0]) + dot_in(cells[1], v.kernel_all[1])
        place_in(v.feed_send, first, first + 2, whole.astype(BF16))
        line_step()
    pixels_sent = send_back("pixels", v.feed_send, v.feed_got)

    arrived(merge_back)
    line_ready(chunks - 1, lambda: jnp.sum(v.merge_pieces[...].astype(F32), axis=0))
    arrived(heads_back)
    v.heads_rows[row] = jnp.sum(v.heads_pieces[...].astype(F32), axis=0).astype(BF16)
    heads_rows = to_rows("heads_rows", lambda there: v.heads_rows.at[row], v.heads_rows.at[row])
    line_step()

    own_part = v.normed_two_send[row].astype(F32)

    @pl.when(is_end)
    def _():
        normed_out().wait_recv()
        v.after_attend[...] = own_part + v.patches_all[rows - 1].astype(F32)

    @pl.when(is_middle)
    def _():
        normed_in(2, near).wait_recv()
        normed_over(1, over).wait_recv()
        others = v.patches_all[2].astype(F32) + v.normed_two_got[1].astype(F32)
        v.after_attend[...] = own_part + others

    normed_grad = v.after_attend[...]
    hat, scale = normal(v.patches[...].astype(F32))
    v.attend_grad[...] += norm_back(hat, scale, v.gains[0:1], normed_grad)
    saved = [fetch(6 + half, v.attend_grad, v.patch_gradient)]
    v.norm_here[pl.ds(0, 1), :] = jnp.sum(normed_grad * hat, axis=0, keepdims=True)
    v.norm_here[pl.ds(1, 1), :] = jnp.sum(normed_grad, axis=0, keepdims=True)
    v.norm_send[...] = jnp.zeros_like(v.norm_send)
    for there in range(team):
        lanes = pl.ds(there * share, share)
        v.norm_send[there, pl.ds(0, 4), pl.ds(0, share)] = v.norm_here[pl.ds(0, 4), lanes]
    v.norm_back[at] = v.norm_send[at]
    norm_back_sent = []
    for step in range(1, team):
        there = turn(at, step, team)
        made = link("norm_back", step, v.norm_send.at[there], v.norm_back.at[at], on_team(step))
        norm_back_sent.append(start(made))
    line_step()
    arrived(norm_back_sent)
    v.norm_rows[row] = jnp.sum(v.norm_back[...], axis=0)
    norm_rows = to_rows("norm_rows", lambda there: v.norm_rows.at[row], v.norm_rows.at[row])

    while done_over[0] < chunks:
        line_step()

    arrived(pixels_sent)
    v.pixels_here[...] = jnp.sum(v.feed_got[...].astype(F32), axis=0).astype(BF16)
    saved.append(fetch(7 + half, v.pixels_here, v.pixels))
    arrived(expand_back)
    for chip in range(half):
        columns = pl.ds(chip * width, width)
        saved.append(fetch(8 + half + chip, v.expand_pieces.at[chip], v.expand_out.at[:, columns]))

    @pl.when(is_end)
    def _():
        for j in range(chunks):
            if not half <= j < 2 * half:
                line_outward(j).wait_recv()

    saved.append(fetch(8 + 2 * half, v.shrink_here, v.shrink_out))
    saved.append(fetch(9 + 2 * half, v.kernel_here, v.kernel_out))
    saved.append(fetch(10 + 2 * half, v.merge_here, v.merge_out))
    arrived(heads_rows)
    for there in range(rows):
        for part in range(3):
            into = pl.ds(part * width + there * head_part, head_part)
            v.heads_here[:, into] = v.heads_rows[there, :, pl.ds(part * head_part, head_part)]
    saved.append(fetch(11 + 2 * half, v.heads_here, v.heads_out))
    arrived(norm_rows)
    v.norm_out[...] = jnp.sum(v.norm_rows[...], axis=0)
    for each in started:
        each.wait_send()

    @pl.when(is_end)
    def _():
        for index, there in enumerate((far, over, near)):
            normed_in(index, there).wait_send()
        for j in range(chunks):
            line_inward(j).wait_send()

    @pl.when(is_middle)
    def _():
        for index, there in enumerate((far, over)):
            normed_over(index, there).wait_send()
        normed_out().wait_send()
        for j in range(chunks):
            line_over(j).wait_send()
            line_outward(j).wait_send()

    for each in saved:
        each.wait()


def layer(given, rows, half, share, grid_cols, heads_here, collective_id):
    local, width = given["patches"].shape
    length = rows * local
    block = width // half
    head_part = width // rows
    ff_part = FF // half
    own_rows = half * share
    team = 2 * half
    chunks = 2 * half + 10
    tall = local + 2 * grid_cols
    wide_taps = -(-9 * share // 128) * 128
    vmem = pl.BlockSpec(memory_space=pltpu.VMEM)

    def low(*shape):
        return pltpu.VMEM(shape, BF16)

    def wide(*shape):
        return pltpu.VMEM(shape, F32)

    def out(dtype, *shape):
        return jax.ShapeDtypeStruct(shape, dtype)

    results = dict(
        pixels=out(BF16, local, width),
        patch_gradient=out(F32, local, width),
        heads_out=out(BF16, share, 3 * width),
        merge_out=out(BF16, share, width),
        expand_out=out(BF16, share, FF),
        shrink_out=out(BF16, own_rows, width),
        kernel_out=out(BF16, 9, share, width),
        norm_out=out(F32, 8, 128),
    )
    piece = (half, local, width)
    back = (half, share, width)
    heads_back = (half, share, 3 * head_part)
    line = (chunks, share, width)
    scratch = dict(
        patches_all=low(rows, local, width),
        norm_low=wide(8, 128),
        heads_low=low(share, 3 * head_part),
        heads_all=low(width, 3 * head_part),
        norm_got=wide(team, 8, 128),
        gains=wide(8, width),
        grads_all=low(*piece),
        usable=low(local, 128),
        key_valid=wide(1, length),
        usable_all=low(half, local, 128),
        merge_low=low(share, width),
        merge_all=low(width, width),
        expand_all=low(width, ff_part),
        kernel_all=low(2, wide_taps, width),
        grads_other=low(*piece),
        shrink_all=low(ff_part, width),
        normed=low(length, width),
        normed_turned=low(width, length),
        attended_turned=low(width, local),
        projected=low(length, 3 * head_part),
        probs=wide(heads_here, length, length),
        attended_send=low(rows, local, head_part),
        attended_got=low(rows, local, head_part),
        attended=low(local, width),
        rim_up_send=low(half, grid_cols, block),
        rim_down_send=low(half, grid_cols, block),
        rim_above=low(half, grid_cols, block),
        rim_below=low(half, grid_cols, block),
        feed_part=wide(half, local, block),
        after_attend=wide(local, width),
        normed_two=low(*piece),
        down_got=low(half, half, local, block),
        down_in=low(*piece),
        slope=wide(half, local, ff_part),
        active=low(half, local, ff_part),
        hidden_grad=low(half, local, ff_part),
        feed_send=low(*piece),
        feed_got=low(*piece),
        normed_two_send=low(*piece),
        normed_two_got=low(*piece),
        grad=wide(ff_part, width),
        shrink_send=low(own_rows, width),
        shrink_got=low(own_rows, width),
        expand_kept=wide(half, share, ff_part),
        expand_send=low(half, share, ff_part),
        expand_got=low(half, share, ff_part),
        expand_sum=low(half, share, ff_part),
        expand_pieces=low(half, share, ff_part),
        cells_send=low(half, local, block),
        cells_got=low(half, local, block),
        above_got=low(half, grid_cols, block),
        below_got=low(half, grid_cols, block),
        norm_here=wide(8, width),
        attend_grad=wide(local, width),
        attended_grad_send=low(rows, local, head_part),
        attended_grad_got=low(rows, local, head_part),
        merge_pieces=low(*back),
        window=low(2, half, local, wide_taps),
        window_other=low(half, local, wide_taps),
        cells_pair=low(half, tall, share),
        cells_other=low(half, tall, share),
        kernel_kept=wide(9, share, width),
        score_grad=low(length, length),
        projected_grad=low(length, 3 * head_part),
        heads_send=low(*heads_back),
        heads_got=low(*heads_back),
        heads_pieces=low(*heads_back),
        heads_rows=low(rows, share, 3 * head_part),
        norm_send=wide(team, 8, 128),
        norm_back=wide(team, 8, 128),
        norm_rows=wide(rows, 8, 128),
        line_got=low(*line),
        send_sem=pltpu.SemaphoreType.DMA((len(KINDS), team)),
        recv_sem=pltpu.SemaphoreType.DMA((len(KINDS), team)),
        pair_send=pltpu.SemaphoreType.DMA((len(PAIRS), 9)),
        pair_recv=pltpu.SemaphoreType.DMA((len(PAIRS), 9)),
        line_send=pltpu.SemaphoreType.DMA((3, chunks)),
        own_sem=pltpu.SemaphoreType.DMA((12 + 2 * half,)),
        pixels_here=low(local, width),
        heads_here=low(share, 3 * width),
        merge_here=low(share, width),
        shrink_here=low(own_rows, width),
        kernel_here=low(9, share, width),
        line_recv=pltpu.SemaphoreType.DMA((3, chunks)),
    )
    outside = ("heads", "merge", "expand", "shrink", "kernel")
    names = tuple(given) + tuple(results) + tuple(scratch)
    values = pl.pallas_call(
        functools.partial(layer_body, (rows, half, share, grid_cols, heads_here), names),
        out_shape=list(results.values()),
        in_specs=[
            pl.BlockSpec(memory_space=pl.ANY)
            if name in outside
            else pl.BlockSpec(memory_space=pltpu.SMEM)
            if name == "widths"
            else vmem
            for name in given
        ],
        out_specs=[
            vmem if name == "norm_out" else pl.BlockSpec(memory_space=pl.ANY) for name in results
        ],
        scratch_shapes=list(scratch.values()),
        compiler_params=pltpu.CompilerParams(
            collective_id=collective_id, has_side_effects=True, vmem_limit_bytes=62 << 20
        ),
        cost_estimate=pl.CostEstimate(
            flops=75 * local * width * width,
            bytes_accessed=16 << 20,
            transcendentals=heads_here * length * length,
        ),
        name="layer",
    )(*given.values())
    return dict(zip(results, values))


def per_device(
    patches,
    pixel_grads,
    widths,
    patch_mask,
    heads_weight,
    heads_first,
    heads_second,
    merge_weight,
    merge_first,
    merge_second,
    expand_weight,
    expand_first,
    expand_second,
    shrink_weight,
    shrink_first,
    shrink_second,
    kernel_weight,
    kernel_first,
    kernel_second,
    norm_table,
    norm_first,
    norm_second,
):
    images, grid_rows, grid_cols, width = patches.shape
    rows, cols = lax.axis_size("row"), TEAM
    teams = lax.axis_size("col") // TEAM
    half = cols // 2
    local = images * grid_rows * grid_cols
    share = width // cols
    heads_here = HEADS // rows

    places = [[at * teams + team for team in range(teams)] for at in range(TEAM)]

    def joined(array, axis):
        if teams == 1:
            return array
        return lax.all_gather(array, "col", axis_index_groups=places, axis=axis, tiled=True)

    def scattered(array, axis):
        if teams == 1:
            return array
        return lax.psum_scatter(
            array, "col", axis_index_groups=places, scatter_dimension=axis, tiled=True
        )

    def held(array, axis):
        return array if teams == 1 else joined(array.astype(BF16), axis).astype(F32)

    found = layer(
        dict(
            patches=patches.reshape(local, width),
            grads=pixel_grads.reshape(local, width),
            heads=held(heads_weight, 0),
            norm_table=held(norm_table, 1),
            widths=widths,
            patch_mask=patch_mask.reshape(patch_mask.shape[1:]),
            merge=held(merge_weight, 0),
            expand=held(expand_weight, 0),
            shrink=held(shrink_weight, 0),
            kernel=held(kernel_weight, 1),
        ),
        rows,
        half,
        share,
        grid_cols,
        heads_here,
        1,
    )
    def share_sum(name, axis):
        return scattered(found[name].astype(F32), axis) if teams > 1 else found[name]

    norm_sum = found["norm_out"]
    if teams > 1:
        norm_sum = scattered(norm_sum[:4, :share], 1)
        norm_sum = jnp.pad(norm_sum, ((0, 4), (0, -norm_sum.shape[1] % 128)))
    values = adam_all(
        [
            (share_sum("heads_out", 0), heads_weight, heads_first, heads_second),
            (share_sum("merge_out", 0), merge_weight, merge_first, merge_second),
            (share_sum("expand_out", 0), expand_weight, expand_first, expand_second),
            (share_sum("shrink_out", 0), shrink_weight, shrink_first, shrink_second),
            (share_sum("kernel_out", 1), kernel_weight, kernel_first, kernel_second),
        ],
        (norm_sum, norm_table, norm_first, norm_second),
        (found["pixels"], found["patch_gradient"]),
    )
    *updated, pixels, patch_gradient = values
    return (pixels.reshape(patches.shape), patch_gradient.reshape(patches.shape), *updated)


def solution(mesh):
    tokens_at = P("col", "row", None, None)
    flat_at = P("col", None)
    kernel_at = P(None, "col", None)
    norm_at = P(None, "col")
    return jax.shard_map(
        per_device,
        mesh=mesh,
        in_specs=(tokens_at, tokens_at, P("col"), P("col", None, None))
        + (flat_at,) * 12
        + (kernel_at,) * 3
        + (norm_at,) * 3,
        out_specs=(tokens_at, tokens_at) + (flat_at,) * 20 + (kernel_at,) * 5 + (norm_at,) * 5,
        check_vma=False,
    )
```
